512 devices in a mesh: dp: 32 (over y, z_lo), tp: 16 (over z_hi, x, core).
Axes of the slice: x: 4, y: 4, z: 16 (z_hi: 2, z_lo: 8; z = z_hi * 8 + z_lo), core: 2. Of those that a mesh axis runs over, the one named last changes fastest.
Arguments:
- clean_latents: bfloat16 [32, 256, 3072], P('dp'), may hold values from -6 to 6
- noise: bfloat16 [32, 256, 3072], P('dp'), may hold values from -6 to 6
- time_index: int32 [32], P('dp'), may hold values from 0 to 999
- teacher_weights: bfloat16 [3072, 8192], P('dp', 'tp'), may hold values from -16 to 16, as said below
- student_weights: bfloat16 [3072, 8192], P('dp', 'tp'), may hold values from -16 to 16, as said below
- teacher_time: bfloat16 [256, 2048], P(None, 'tp'), may hold values from -0.375 to 0.375
- student_time: bfloat16 [256, 2048], P(None, 'tp'), may hold values from -0.375 to 0.375
Outputs:
- student_velocity: bfloat16 [32, 256, 3072], P('dp', 'tp')
- student_grad: bfloat16 [3072, 8192], P('dp', 'tp')
The draws below stay inside these ranges and needn't reach their ends.
Inputs may be any that keep to these rules, and one draw needn't show every extreme that they name: `teacher_weights`: packed attention weights, per head query, key, value and output blocks. `student_weights`: packed attention weights, per head query, key, value and output blocks.
All inputs are finite; a program needn't handle non-finite values.
Results may differ from the reference program's by a relative error of at most 0.033.
Values may be sent and summed in bfloat16 or wider, within the bound.
A program may use at most 128 MiB of HBM per device.

```python
import math
import jax
import jax.numpy as jnp
from jax import lax

D = 3072
HD = 128
FREQ = 256
SEQ = 256
STEPS = 1000
HEADS = 16
IMAGES = 32


def packed_block(key):
    subkeys = jax.random.split(key, 2)
    projections = jax.random.truncated_normal(subkeys[0], -6.0, 6.0, (D, HEADS, 3, HD), jnp.float32) * D ** (-0.5)
    output = jax.random.truncated_normal(subkeys[1], -6.0, 6.0, (D, HEADS, HD), jnp.float32) * (HEADS * HD) ** (-0.5)
    queries = projections[:, :, 0]
    key_columns = projections[:, :, 1]
    packed = jnp.stack([queries, key_columns, projections[:, :, 2], output], axis=2)
    return packed.reshape(D, HEADS * 4 * HD).astype(jnp.bfloat16)


def draw_teacher_weights(key, part):
    key = jax.random.fold_in(key, 11)
    return packed_block(key)


def draw_student_weights(key, part):
    key = jax.random.fold_in(key, 23)
    return packed_block(key)


def touch_ends(array, key, least, high):
    longest = array.shape.index(max(array.shape))
    spots = []
    for shift in (0, 1):
        where = [jax.random.randint(jax.random.fold_in(key, axis), (), 0, length) for axis, length in enumerate(array.shape)]
        where[longest] = (where[longest] + shift) % array.shape[longest]
        spots.append(tuple(where))
    return array.at[spots[0]].set(least).at[spots[1]].set(high)


def with_spikes(array, stream_key, source, target, blocks, factor):
    def block_of(dim):
        return (jnp.arange(array.shape[dim]) // (array.shape[dim] // blocks)).reshape((-1,) + (1,) * (array.ndim - 1 - dim))

    first = jax.random.permutation(stream_key, blocks)[block_of(target)]
    other_side = (block_of(target) + blocks // 2) % blocks
    return jnp.where((block_of(source) == first) | (block_of(source) == other_side), factor * array, array)


def shard_levels(key, dims, shards, least, largest):
    loudness, own = 1.0, jax.random.fold_in(key, 6)
    for dim, blocks in shards:
        draws = jnp.exp(jax.random.uniform(jax.random.fold_in(own, dim), (blocks,), jnp.float32, least / len(shards), largest / len(shards)))
        loudness = loudness * jnp.repeat(draws, dims[dim] // blocks).reshape([-1 if axis == dim else 1 for axis in range(len(dims))])
    return loudness


def normal_values(own_key, shape, scale, reach, shards=(), kind=jnp.bfloat16):
    result = scale * jax.random.normal(own_key, shape, jnp.float32)
    if shards:
        result = result * shard_levels(own_key, shape, shards, -0.22, 0.18)
    return jnp.clip(result, -reach, reach).astype(kind)


def heavy_noise(stream_key, shape, scale, limit, cuts, heavy, kind=jnp.bfloat16):
    values = scale * jax.random.normal(stream_key, shape, jnp.float32)
    if cuts:
        values = values * shard_levels(stream_key, shape, cuts, -0.22, 0.18)
    return jnp.clip(with_spikes(values, jax.random.fold_in(stream_key, 3), *heavy), -limit, limit).astype(kind)


def setup_inputs(seed: int = 0) -> dict:
    keys = jax.random.split(jax.random.key(seed), 8)
    return {
        "clean_latents": heavy_noise(keys[0], (IMAGES, SEQ, D), 1.0, 6.0, ((0, 32),), (0, 2, 32, 2.75)),
        "noise": normal_values(keys[1], (IMAGES, SEQ, D), 1.0, 6.0, ((0, 32),)),
        "time_index": touch_ends(jax.random.randint(keys[2], (IMAGES,), 0, STEPS), jax.random.fold_in(keys[2], 1), 0, STEPS - 1).astype(jnp.int32),
        "teacher_weights": draw_teacher_weights(jax.random.fold_in(keys[7], 71), 0),
        "student_weights": draw_student_weights(jax.random.fold_in(keys[7], 71), 0),
        "teacher_time": normal_values(keys[5], (FREQ, HEADS * HD), FREQ ** -0.5, 0.375, ((1, 16),)),
        "student_time": normal_values(keys[6], (FREQ, HEADS * HD), FREQ ** -0.5, 0.375, ((1, 16),)),
    }


def plan_time(time_step):
    return 0.05 + 1.45 * (time_step.astype(jnp.float32) + 0.5) / STEPS

def time_embedding(step_time, width):
    half_width = width // 2
    position = jnp.arange(half_width, dtype=jnp.float32)
    frequencies = 4.0 * jnp.exp(-jnp.log(100.0) * position / half_width)
    phases = step_time * frequencies
    time_features = jnp.concatenate([jnp.cos(phases), jnp.sin(phases)])
    time_slope = jnp.concatenate([-frequencies * jnp.sin(phases), frequencies * jnp.cos(phases)])
    return (time_features, time_slope)

def keep_bfloat(values):
    return lax.optimization_barrier(values.astype(jnp.bfloat16)).astype(jnp.float32)

def head_forward(normed_b, weight_block, gate_vec):
    head_size = weight_block.shape[1] // 4
    score_scale = head_size ** (-0.5)
    projections = jnp.dot(normed_b, weight_block[:, :3 * head_size], preferred_element_type=jnp.float32).astype(jnp.bfloat16)
    queries = projections[:, :head_size]
    key_rows = projections[:, head_size:2 * head_size]
    values = projections[:, 2 * head_size:]
    scores = jnp.dot(queries, key_rows.T, preferred_element_type=jnp.float32) * score_scale
    attention = jax.nn.softmax(scores, axis=-1)
    attention_b = attention.astype(jnp.bfloat16)
    attended = jnp.dot(attention_b, values, preferred_element_type=jnp.float32)
    gated = (attended * (1.0 + gate_vec)).astype(jnp.bfloat16)
    head_term = jnp.dot(gated, weight_block[:, 3 * head_size:].T, preferred_element_type=jnp.float32)
    return (head_term, (queries, key_rows, values, attention, attention_b, attended, gated))

def head_tangent(d_normed_b, weight_block, gate_vec, gate_slope, stashed):
    queries, key_rows, values, attention, attention_b, attended, gated = stashed
    head_size = weight_block.shape[1] // 4
    score_scale = head_size ** (-0.5)
    d_proj = jnp.dot(d_normed_b, weight_block[:, :3 * head_size], preferred_element_type=jnp.float32).astype(jnp.bfloat16)
    d_queries = d_proj[:, :head_size]
    d_keys = d_proj[:, head_size:2 * head_size]
    d_values = d_proj[:, 2 * head_size:]
    d_scores = (jnp.dot(d_queries, key_rows.T, preferred_element_type=jnp.float32) + jnp.dot(queries, d_keys.T, preferred_element_type=jnp.float32)) * score_scale
    d_attention = attention * (d_scores - lax.optimization_barrier(jnp.sum(attention * d_scores, axis=-1, keepdims=True)))
    d_attention_b = d_attention.astype(jnp.bfloat16)
    d_attended = jnp.dot(d_attention_b, values, preferred_element_type=jnp.float32) + jnp.dot(attention_b, d_values, preferred_element_type=jnp.float32)
    d_gated = (d_attended * (1.0 + gate_vec) + attended * gate_slope).astype(jnp.bfloat16)
    return jnp.dot(d_gated, weight_block[:, 3 * head_size:].T, preferred_element_type=jnp.float32)

def head_backward(normed_b, cotangent_b, weight_block, gate_vec, stashed):
    queries, key_rows, values, attention, attention_b, attended, gated = stashed
    head_size = weight_block.shape[1] // 4
    score_scale = head_size ** (-0.5)
    grad_out = jnp.dot(cotangent_b.T, gated, preferred_element_type=jnp.float32)
    d_gated = jnp.dot(cotangent_b, weight_block[:, 3 * head_size:], preferred_element_type=jnp.float32)
    d_att_b = (d_gated * (1.0 + gate_vec)).astype(jnp.bfloat16)
    grad_values = jnp.dot(attention_b.T, d_att_b, preferred_element_type=jnp.float32)
    d_back = jnp.dot(d_att_b, values.T, preferred_element_type=jnp.float32)
    d_scores_b = (attention * (d_back - lax.optimization_barrier(jnp.sum(attention * d_back, axis=-1, keepdims=True))) * score_scale).astype(jnp.bfloat16)
    grad_queries = jnp.dot(d_scores_b, key_rows, preferred_element_type=jnp.float32)
    grad_keys = jnp.dot(d_scores_b.T, queries, preferred_element_type=jnp.float32)
    d_proj_b = jnp.concatenate([grad_queries, grad_keys, grad_values], axis=1).astype(jnp.bfloat16)
    grad_proj = jnp.dot(normed_b.T, d_proj_b, preferred_element_type=jnp.float32)
    return jnp.concatenate([grad_proj, grad_out], axis=1)

def reference(clean_latents, noise, time_index, teacher_weights, student_weights, teacher_time, student_time):
    teacher_blocks = teacher_weights.reshape(D, HEADS, 4 * HD).transpose(1, 0, 2)
    student_blocks = student_weights.reshape(D, HEADS, 4 * HD).transpose(1, 0, 2)
    teacher_tables = teacher_time.reshape(FREQ, HEADS, HD).transpose(1, 0, 2)
    student_tables = student_time.reshape(FREQ, HEADS, HD).transpose(1, 0, 2)
    factor = math.sqrt(D / IMAGES)

    def one_image(running_sum, image_item):
        latent_rows, noise_rows, time_step = image_item
        step_time = plan_time(time_step)
        cosine = jnp.cos(step_time)
        sine = jnp.sin(step_time)
        noisy = cosine * latent_rows.astype(jnp.float32) + sine * noise_rows.astype(jnp.float32)
        inv_rms = lax.rsqrt(lax.optimization_barrier(jnp.mean(noisy * noisy, axis=-1, keepdims=True)) + 1e-06)
        normed = noisy * inv_rms
        normed_b = normed.astype(jnp.bfloat16)
        time_features, time_slope = time_embedding(step_time, FREQ)
        zeros_field = jnp.zeros((SEQ, D), jnp.float32)

        def teacher_head(accumulated, weight_pair):
            weight_block, time_table = weight_pair
            gate_vec = jnp.dot(time_features, time_table.astype(jnp.float32), precision=lax.Precision.HIGHEST)
            head_term = head_forward(normed_b, weight_block, gate_vec)[0]
            return (accumulated + keep_bfloat(head_term), None)
        teacher_total = lax.scan(teacher_head, zeros_field, (teacher_blocks, teacher_tables))[0]
        velocity = (noisy + teacher_total).astype(jnp.bfloat16)
        tangent = velocity.astype(jnp.float32)
        d_normed = inv_rms * (tangent - normed * lax.optimization_barrier(jnp.mean(normed * tangent, axis=-1, keepdims=True)))
        d_normed_b = d_normed.astype(jnp.bfloat16)

        def student_head(carry, weight_pair):
            term_acc, d_acc = carry
            weight_block, time_table = weight_pair
            table_f = time_table.astype(jnp.float32)
            gate_vec = jnp.dot(time_features, table_f, precision=lax.Precision.HIGHEST)
            gate_slope = jnp.dot(time_slope, table_f, precision=lax.Precision.HIGHEST)
            head_term, stashed = head_forward(normed_b, weight_block, gate_vec)
            d_term = head_tangent(d_normed_b, weight_block, gate_vec, gate_slope, stashed)
            return ((term_acc + keep_bfloat(head_term), d_acc + keep_bfloat(d_term)), stashed)
        (term_total, d_total), stashed_all = lax.scan(student_head, (zeros_field, zeros_field), (student_blocks, student_tables))
        predicted = noisy + term_total
        d_predicted = tangent + d_total
        target_gap = -(cosine * cosine) * (predicted - tangent) - cosine * sine * (noisy + d_predicted)
        gap_norm = jnp.sqrt(jnp.sum(target_gap * target_gap))
        cotangent = target_gap * (-factor / (gap_norm + 0.1))
        cotangent_b = cotangent.astype(jnp.bfloat16)

        def backward_head(stored):
            weight_block, time_table, stashed = stored
            gate_vec = jnp.dot(time_features, time_table.astype(jnp.float32), precision=lax.Precision.HIGHEST)
            return head_backward(normed_b, cotangent_b, weight_block, gate_vec, stashed).astype(jnp.bfloat16)
        head_grads = lax.map(backward_head, (student_blocks, student_tables, stashed_all))
        image_grad = head_grads.transpose(1, 0, 2).reshape(D, HEADS * 4 * HD)
        return (running_sum + lax.optimization_barrier(image_grad).astype(jnp.float32), predicted.astype(jnp.bfloat16))
    initial = jnp.zeros((D, HEADS * 4 * HD), jnp.float32)
    grad_total, predictions = lax.scan(one_image, initial, (clean_latents, noise, time_index))
    return (predictions, grad_total.astype(jnp.bfloat16))
```

```python
import functools
import math

import jax
import jax.numpy as jnp
from jax import lax
from jax.experimental import pallas as pl
from jax.experimental.pallas import tpu as pltpu
from jax.sharding import PartitionSpec as P

D = 3072
HD = 128
STEPS = 1000
IMAGES = 32
NY, NZ, NX = 4, 8, 4
CH = 4
CW = D // CH
ROWS = D // IMAGES
HALF = ROWS // 2
SEQ = 256
OWN = 16
BF = jnp.bfloat16
F32 = jnp.float32
MESH = pl.DeviceIdType.MESH


def mm(a, b):
    return jnp.dot(a, b, preferred_element_type=F32)


def mm_t(a, b):
    return lax.dot_general(a, b, (((1,), (1,)), ((), ())), preferred_element_type=F32)


def t_mm(a, b):
    return lax.dot_general(a, b, (((0,), (0,)), ((), ())), preferred_element_type=F32)


def kernel(
    time_ref,
    clean_hbm,
    noise_hbm,
    wt_hbm,
    ws_hbm,
    tt_hbm,
    ts_hbm,
    out_v,
    out_g,
    clean,
    noise,
    tables,
    w,
    noisy,
    normed,
    inv,
    trig,
    gates,
    acc,
    proj,
    att,
    att_b,
    attended,
    gated,
    term,
    s_term,
    g_term,
    core_in,
    x_sum,
    x_in,
    z_sum,
    z_in,
    vel,
    gap,
    dnorm,
    grad,
    y_half,
    y_full,
    z_flow,
    load_sem,
    wz_s,
    wz_r,
    wy_s,
    wy_r,
    wh_s,
    wh_r,
    c_s,
    c_r,
    x_s,
    x_r,
    z_s,
    z_r,
    ax_s,
    ax_r,
    ac_s,
    ac_r,
    gh_s,
    gh_r,
    gf_s,
    gf_r,
    gz_s,
    gz_r,
):
    dp, tp = lax.axis_index("dp"), lax.axis_index("tp")
    y, zl = dp // NZ, dp % NZ
    zh, x, c = tp // (2 * NX), (tp // 2) % NX, tp % 2

    def at(yy, zz, hh, xx, cc):
        return (yy * NZ + zz, hh * 2 * NX + xx * 2 + cc)

    def y_to(k):
        return at((y + k + NY) % NY, zl, zh, x, c)

    def z_to(k):
        z = (zh * NZ + zl + k + 2 * NZ) % (2 * NZ)
        return at(y, z % NZ, z // NZ, x, c)

    def x_to(k):
        return at(y, zl, zh, (x + k + NX) % NX, c)

    core_dev = at(y, zl, zh, x, 1 - c)
    far_dev = at(y, zl, 1 - zh, x, c)

    def rcopy(src, dst, send, recv, device):
        return pltpu.make_async_remote_copy(
            src_ref=src, dst_ref=dst, send_sem=send, recv_sem=recv, device_id=device, device_id_type=MESH
        )

    loads = []
    n_load = 0
    for j in range(CH):
        for src, dst in ((clean_hbm, clean), (noise_hbm, noise)):
            loads.append(
                pltpu.make_async_copy(src.at[:, pl.ds(j * CW, CW)], dst.at[j], load_sem.at[n_load])
            )
            n_load += 1
    for m, src in enumerate((tt_hbm, ts_hbm)):
        loads.append(pltpu.make_async_copy(src, tables.at[m], load_sem.at[n_load]))
        n_load += 1
    w_hbm = (wt_hbm, ws_hbm)
    own_w = []
    for m in range(2):
        own_w.append(pltpu.make_async_copy(w_hbm[m], w.at[m, dp], load_sem.at[n_load]))
        n_load += 1
    for copy in own_w + loads:
        copy.start()

    barrier = pltpu.get_barrier_semaphore()
    partners = [z_to(1), z_to(-1), y_to(1), y_to(-1), core_dev, x_to(1), x_to(2), x_to(3), far_dev]
    for device in partners:
        pl.semaphore_signal(barrier, inc=1, device_id=device, device_id_type=MESH)
    pl.semaphore_wait(barrier, len(partners))

    def wblk(m, yy, o):
        return w.at[m, ((yy + NY) % NY) * NZ + o]

    def wz_copy(m, o, way, src=None):
        blk = wblk(m, y, o)
        return rcopy(blk if src is None else src, blk, wz_s.at[m, o, way], wz_r.at[m, o], z_to(1 - 2 * way))

    def wy_copy(m, o, way, src=None):
        blk = wblk(m, y, o)
        return rcopy(blk if src is None else src, blk, wy_s.at[m, o, way], wy_r.at[m, o, way], y_to(1 - 2 * way))

    def wy_arrival(m, o, way):
        blk = wblk(m, y - 1 + 2 * way, o)
        return rcopy(blk, blk, wy_s.at[m, o, way], wy_r.at[m, o, way], y_to(1 - 2 * way))

    def wh_copy(m, o, way):
        blk = wblk(m, y - 1 + 2 * way, o).at[pl.ds(way * HALF, HALF)]
        return rcopy(blk, blk, wh_s.at[m, o, way], wh_r.at[m, o, way], y_to(1 - 2 * way))

    def wh_arrival(m, o, way):
        blk = wblk(m, y + 2, o).at[pl.ds(way * HALF, HALF)]
        return rcopy(blk, blk, wh_s.at[m, o, way], wh_r.at[m, o, way], y_to(1 - 2 * way))

    def w_own(m, with_y):
        @pl.when(zl < NZ - 1)
        def _():
            wz_copy(m, zl, 0, w_hbm[m]).start()

        @pl.when(zl > 0)
        def _():
            wz_copy(m, zl, 1, w_hbm[m]).start()

        if with_y:
            for way in range(2):
                wy_copy(m, zl, way, w_hbm[m]).start()

    def w_zstep(m, s, with_y):
        for way in range(2):
            o = zl - s if way == 0 else zl + s
            there = o >= 0 if way == 0 else o < NZ
            onward = zl < NZ - 1 if way == 0 else zl > 0

            @pl.when(there)
            def _():
                wz_copy(m, o, way).wait_recv()

                @pl.when(onward)
                def _():
                    wz_copy(m, o, way).start()

                if with_y:
                    for side in range(2):
                        wy_copy(m, o, side).start()

    def w_ystart(m):
        for way in range(2):
            wy_copy(m, zl, way, w_hbm[m]).start()

        def body(s, carry):
            for o, there in ((zl - s, zl - s >= 0), (zl + s, zl + s < NZ)):

                @pl.when(there)
                def _():
                    for side in range(2):
                        wy_copy(m, o, side).start()

            return carry

        lax.fori_loop(1, NZ, body, 0)

    def w_ystep(m, s):
        sides = ((zl, zl >= 0),) if s == 0 else ((zl - s, zl - s >= 0), (zl + s, zl + s < NZ))
        for o, there in sides:

            @pl.when(there)
            def _():
                for way in range(2):
                    wy_arrival(m, o, way).wait_recv()
                    wh_copy(m, o, way).start()

    def w_hwait(m):
        def body(o, carry):
            for way in range(2):
                wh_arrival(m, o, way).wait_recv()
            return carry

        lax.fori_loop(0, NZ, body, 0)
        own_w[m].wait()

    def w_drain(m):
        def body(o, carry):
            @pl.when((o <= zl) & (zl < NZ - 1))
            def _():
                wz_copy(m, o, 0).wait_send()

            @pl.when((o >= zl) & (zl > 0))
            def _():
                wz_copy(m, o, 1).wait_send()

            for way in range(2):
                wy_copy(m, o, way).wait_send()
                wh_copy(m, o, way).wait_send()
            return carry

        lax.fori_loop(0, NZ, body, 0)

    def cs_copy(n, buf, j):
        return rcopy(buf.at[j, :, :, 1 - c], core_in.at[n, j], c_s.at[n, j], c_r.at[n, j], core_dev)

    def xs_copy(n, j, k):
        return rcopy(
            x_sum.at[n, j, :, (x + k) % NX], x_in.at[n, j, k - 1], x_s.at[n, j, k - 1], x_r.at[n, j, k - 1], x_to(k)
        )

    def zs_copy(n, j):
        if n == 2:
            return rcopy(z_sum.at[n, j, 1 - zh], z_in.at[n, j, zh], z_s.at[n, j], z_r.at[n, j], far_dev)
        return rcopy(z_sum.at[n, j], z_in.at[n, j], z_s.at[n, j], z_r.at[n, j], far_dev)

    def zs_arrival(n, j):
        if n == 2:
            return rcopy(z_sum.at[n, j, zh], z_in.at[n, j, 1 - zh], z_s.at[n, j], z_r.at[n, j], far_dev)
        return zs_copy(n, j)

    def ax_copy(n, buf, j, k):
        mine = buf.at[j, :, x, c]
        return rcopy(mine, mine, ax_s.at[n, j, k - 1], ax_r.at[n, j, k - 1], x_to(k))

    def ax_arrival(n, buf, j, k):
        blk = buf.at[j, :, (x + NX - k) % NX, c]
        return rcopy(blk, blk, ax_s.at[n, j, k - 1], ax_r.at[n, j, k - 1], x_to(k))

    def ac_copy(n, buf, j, k, cc):
        blk = buf.at[j, :, (x + NX - k) % NX, cc]
        return rcopy(blk, blk, ac_s.at[n, j, k], ac_r.at[n, j, k], core_dev)

    def sum_x_start(n, buf, j):
        cs_copy(n, buf, j).wait_recv()
        for hh in range(2):
            for xx in range(NX):
                total = buf[j, hh, xx, c].astype(F32) + core_in[n, j, hh, xx].astype(F32)
                x_sum[n, j, hh, xx] = total.astype(BF)
        for k in (2, 1, 3):
            xs_copy(n, j, k).start()

    def sum_z_start(n, j):
        for k in range(1, NX):
            xs_copy(n, j, k).wait_recv()
        for hh in range(2):
            total = x_sum[n, j, hh, x].astype(F32)
            for k in range(NX - 1):
                total = total + x_in[n, j, k, hh].astype(F32)
            z_sum[n, j, hh] = total.astype(BF)
        zs_copy(n, j).start()

    def share_start(n, buf, j):
        for k in (2, 1, 3):
            ax_copy(n, buf, j, k).start()
        ac_copy(n, buf, j, 0, c).start()

    def share_forward(n, buf, j):
        for k in (1, 3, 2):
            ax_arrival(n, buf, j, k).wait_recv()
            ac_copy(n, buf, j, k, c).start()

    def share_wait(n, buf, j):
        for k in range(NX):
            ac_copy(n, buf, j, k, 1 - c).wait_recv()

    def sum_drain(n, buf, shared):
        for j in range(CH):
            cs_copy(n, buf, j).wait_send()
            for k in range(1, NX):
                xs_copy(n, j, k).wait_send()
            zs_copy(n, j).wait_send()
            if shared is not None:
                for k in range(1, NX):
                    ax_copy(n, shared, j, k).wait_send()
                for k in range(NX):
                    ac_copy(n, shared, j, k, c).wait_send()

    def project(src, m):
        acc[...] = jnp.zeros_like(acc)

        @pl.loop(0, CH)
        def _(j):
            left = src[j].reshape(SEQ, CW)
            right = w[m, pl.ds(NZ * j, NZ), :, 0 : 3 * HD].reshape(CW, 3 * HD)
            acc[...] += mm(left, right)

        return acc[...].astype(BF)

    scale = HD ** (-0.5)

    def forward(m):
        proj[...] = project(normed, m)
        queries, keys, values = (proj[:, i * HD : (i + 1) * HD] for i in range(3))
        scores = mm_t(queries, keys) * scale
        top = jnp.max(scores, axis=-1, keepdims=True)
        raised = jnp.exp(scores - top)
        probs = raised / jnp.sum(raised, axis=-1, keepdims=True)
        att[...] = probs
        att_b[...] = probs.astype(BF)
        attended[...] = mm(att_b[...], values)
        gated[...] = (attended[...] * (1.0 + gates[pl.ds(m, 1)])).astype(BF)

    def out_columns(m, j):
        return w[m, pl.ds(NZ * j, NZ), :, 3 * HD :].reshape(CW, HD)

    shape6 = (2, NX, 2, OWN, CW)

    w_own(0, True)
    w_own(1, False)

    for copy in loads:
        copy.wait()
    steps = jnp.full((1, CW), time_ref[0].astype(F32))
    step_time = 0.05 + 1.45 * (steps + 0.5) / STEPS
    trig[pl.ds(0, 1)] = jnp.cos(step_time)
    trig[pl.ds(1, 1)] = jnp.sin(step_time)

    @pl.loop(0, 2 * NX * 2)
    def _(r):
        hh, xx, cc = r // (2 * NX), (r // 2) % NX, r % 2
        cosine, sine = trig[pl.ds(0, 1)], trig[pl.ds(1, 1)]
        square = jnp.zeros((OWN, 1), F32)
        for j in range(CH):
            rows = pl.ds(pl.multiple_of(r * OWN, OWN), OWN)
            mixed = cosine * clean[j, rows].astype(F32) + sine * noise[j, rows].astype(F32)
            noisy[j, hh, xx, cc] = mixed
            square = square + jnp.sum(mixed * mixed, axis=-1, keepdims=True)
        factor = lax.rsqrt(square / D + 1e-06)
        inv[hh, xx, cc] = jnp.broadcast_to(factor, (OWN, HD))
        for j in range(CH):
            normed[j, hh, xx, cc] = (noisy[j, hh, xx, cc] * factor).astype(BF)

    half = tables.shape[1] // 2
    position = lax.broadcasted_iota(jnp.int32, (half, HD), 0).astype(F32)
    frequency = 4.0 * jnp.exp(-math.log(100.0) * position / half)
    phases = step_time[:, :HD] * frequency
    cos_p, sin_p = jnp.cos(phases), jnp.sin(phases)
    for m in range(2):
        low, high = tables[m, :half].astype(F32), tables[m, half:].astype(F32)
        gates[pl.ds(m, 1)] = jnp.sum(cos_p * low + sin_p * high, axis=0, keepdims=True)
        if m == 1:
            gates[pl.ds(2, 1)] = jnp.sum(frequency * (cos_p * high - sin_p * low), axis=0, keepdims=True)

    for s in range(1, NZ):
        w_zstep(0, s, True)
        w_ystep(0, s - 1)
        w_zstep(1, s, False)
    w_ystep(0, NZ - 1)
    w_ystart(1)
    w_hwait(0)

    forward(0)
    for j in range(CH):
        term[j] = mm_t(gated[...], out_columns(0, j)).astype(BF).reshape(shape6)
        cs_copy(0, term, j).start()

    def velocity_rows(j):
        zs_arrival(0, j).wait_recv()
        for hh in range(2):
            total = z_sum[0, j, hh].astype(F32) + z_in[0, j, hh].astype(F32)
            vel[j, hh, x, c] = (noisy[j, hh, x, c] + total).astype(BF)
        share_start(0, vel, j)

    for j in range(CH):
        sum_x_start(0, term, j)
    w_ystep(1, 0)
    for j in range(CH):
        sum_z_start(0, j)
        w_ystep(1, j + 1)
    for j in range(CH):
        velocity_rows(j)
        if j + CH + 1 < NZ:
            w_ystep(1, j + CH + 1)
    for j in range(CH):
        share_forward(0, vel, j)
    w_hwait(1)

    forward(1)
    for j in range(CH):
        s_term[j] = mm_t(gated[...], out_columns(1, j)).astype(BF).reshape(shape6)
    for j in range(CH):
        share_wait(0, vel, j)

    @pl.loop(0, 2 * NX * 2)
    def _(r):
        hh, xx, cc = r // (2 * NX), (r // 2) % NX, r % 2
        factor = inv[hh, xx, cc][:, :1]
        inner = jnp.zeros((OWN, 1), F32)
        for j in range(CH):
            product = noisy[j, hh, xx, cc] * factor * vel[j, hh, xx, cc].astype(F32)
            inner = inner + jnp.sum(product, axis=-1, keepdims=True)
        inner = inner / D
        for j in range(CH):
            whole = noisy[j, hh, xx, cc] * factor
            dnorm[j, hh, xx, cc] = (factor * (vel[j, hh, xx, cc].astype(F32) - whole * inner)).astype(BF)

    d_proj = project(dnorm, 1)
    d_queries, d_keys, d_values = (d_proj[:, i * HD : (i + 1) * HD] for i in range(3))
    d_scores = (mm_t(d_queries, proj[:, HD : 2 * HD]) + mm_t(proj[:, :HD], d_keys)) * scale
    probs = att[...]
    d_probs = probs * (d_scores - jnp.sum(probs * d_scores, axis=-1, keepdims=True))
    d_attended = mm(d_probs.astype(BF), proj[:, 2 * HD :]) + mm(att_b[...], d_values)
    d_gated = (d_attended * (1.0 + gates[1:2]) + attended[...] * gates[2:3]).astype(BF)
    for j in range(CH):
        d_term = mm_t(d_gated, out_columns(1, j)).astype(BF).astype(F32)
        cosine, sine = trig[0:1], trig[1:2]
        both = cosine * cosine * s_term[j].reshape(SEQ, CW).astype(F32) + cosine * sine * d_term
        g_term[j] = both.astype(BF).reshape(shape6)
        cs_copy(1, g_term, j).start()

    def gap_rows(j):
        zs_arrival(1, j).wait_recv()
        cosine, sine = trig[0:1], trig[1:2]
        for hh in range(2):
            total = z_sum[1, j, hh].astype(F32) + z_in[1, j, hh].astype(F32)
            clear = -(cosine * cosine + cosine * sine) * noisy[j, hh, x, c]
            moved = (cosine * cosine - cosine * sine) * vel[j, hh, x, c].astype(F32)
            gap[j, hh, x, c] = (clear + moved - total).astype(BF)
        share_start(1, gap, j)

    for j in range(CH):
        sum_x_start(1, g_term, j)
    for j in range(CH):
        cs_copy(2, s_term, j).start()
    for j in range(CH):
        sum_z_start(1, j)
    for j in range(CH):
        sum_x_start(2, s_term, j)
    for j in range(CH):
        gap_rows(j)
    for j in range(CH):
        share_forward(1, gap, j)
    for j in range(CH):
        sum_z_start(2, j)
    for j in range(CH):
        share_wait(1, gap, j)

    square = jnp.zeros((1, 1), F32)
    back = jnp.zeros((SEQ, HD), F32)
    for j in range(CH):
        whole = gap[j].reshape(SEQ, CW)
        wide = whole.astype(F32)
        rows = jnp.sum(wide * wide, axis=0, keepdims=True)
        square = square + jnp.sum(rows, axis=1, keepdims=True)
        back = back + mm(whole, out_columns(1, j))
    cot = -math.sqrt(D / IMAGES) / (jnp.sqrt(square) + 0.1)
    d_att_b = (back * cot * (1.0 + gates[1:2])).astype(BF)
    queries, keys, values = (proj[:, i * HD : (i + 1) * HD] for i in range(3))
    grad_values = t_mm(att_b[...], d_att_b)
    d_back = mm_t(d_att_b, values)
    probs = att[...]
    d_scores_b = (probs * (d_back - jnp.sum(probs * d_back, axis=-1, keepdims=True)) * scale).astype(BF)
    grad_queries = mm(d_scores_b, keys)
    grad_keys = t_mm(d_scores_b, queries)
    d_proj_b = jnp.concatenate([grad_queries, grad_keys, grad_values], axis=1).astype(BF)

    def gh_copy(d, way):
        part = pl.ds(way * HALF, HALF)
        return rcopy(
            grad.at[(y + 2) % NY, d, part], y_half.at[way, d], gh_s.at[way, d], gh_r.at[way, d], y_to(1 - 2 * way)
        )

    def gf_copy(d, way):
        return rcopy(
            grad.at[(y + 1 - 2 * way + NY) % NY, d],
            y_full.at[way, d],
            gf_s.at[way, d],
            gf_r.at[way, d],
            y_to(1 - 2 * way),
        )

    def gz_copy(d, way):
        return rcopy(grad.at[y, d], z_flow.at[way, d], gz_s.at[d], gz_r.at[way, d], z_to(1 - 2 * way))

    for k in (2, 1, 3, 0):
        yy = (y + k) % NY
        left = t_mm(normed[yy].reshape(SEQ, CW), d_proj_b)
        grad[yy, :, :, 0 : 3 * HD] = left.astype(BF).reshape(NZ, ROWS, 3 * HD)
        right = t_mm(gap[yy].reshape(SEQ, CW), gated[...]) * cot
        grad[yy, :, :, 3 * HD :] = right.astype(BF).reshape(NZ, ROWS, HD)
        if k == 2:

            @pl.loop(0, NZ)
            def _(i):
                d = jnp.where(i % 2 == 0, NZ - 1 - i // 2, i // 2)
                for way in range(2):
                    gh_copy(d, way).start()

    def order(i):
        return jnp.where(i % 2 == 0, NZ - 1 - i // 2, i // 2)

    def reduced(d):
        for way in range(2):
            gf_copy(d, way).wait_recv()
        return grad[y, d].astype(F32) + y_full[0, d].astype(F32) + y_full[1, d].astype(F32)

    @pl.loop(0, 13)
    def _(t):
        @pl.when(t < NZ)
        def _():
            d = order(t)
            for way in range(2):
                gh_copy(d, way).wait_recv()
                yy = (y + 1 - 2 * way + NY) % NY
                part = pl.ds(way * HALF, HALF)
                total = grad[yy, d, part].astype(F32) + y_half[way, d].astype(F32)
                grad[yy, d, part] = total.astype(BF)
                gf_copy(d, way).start()

        for way in range(2):
            hops = zl if way == 0 else NZ - 1 - zl
            i = t - 1 - hops
            ok = (i >= 0) & (i < NZ)
            d = order(jnp.clip(i, 0, NZ - 1))

            @pl.when(ok & ((zl < d) if way == 0 else (zl > d)))
            def _():
                total = reduced(d)

                @pl.when(hops > 0)
                def _():
                    gz_copy(d, way).wait_recv()
                    grad[y, d] = (total + z_flow[way, d].astype(F32)).astype(BF)

                @pl.when(hops == 0)
                def _():
                    grad[y, d] = total.astype(BF)

                gz_copy(d, way).start()

        @pl.when(t == 12)
        def _():
            total = reduced(zl)

            @pl.when(zl > 0)
            def _():
                gz_copy(zl, 0).wait_recv()

            @pl.when(zl < NZ - 1)
            def _():
                gz_copy(zl, 1).wait_recv()

            @pl.when(zl == 0)
            def _():
                out_g[...] = (total + z_flow[1, zl].astype(F32)).astype(BF)

            @pl.when(zl == NZ - 1)
            def _():
                out_g[...] = (total + z_flow[0, zl].astype(F32)).astype(BF)

            @pl.when((zl > 0) & (zl < NZ - 1))
            def _():
                out_g[...] = (total + z_flow[0, zl].astype(F32) + z_flow[1, zl].astype(F32)).astype(BF)

    for j in range(CH):
        zs_arrival(2, j).wait_recv()
        total = z_sum[2, j, zh].astype(F32) + z_in[2, j, 1 - zh].astype(F32)
        out_v[:, j * CW : (j + 1) * CW] = (noisy[j, zh, x, c] + total).astype(BF)

    w_drain(0)
    w_drain(1)
    sum_drain(0, term, vel)
    sum_drain(1, g_term, gap)
    sum_drain(2, s_term, None)

    @pl.loop(0, NZ)
    def _(d):
        for way in range(2):
            gh_copy(d, way).wait_send()
            gf_copy(d, way).wait_send()

        @pl.when(d != zl)
        def _():
            gz_copy(d, 0).wait_send()


def on_device(clean, noise, time_index, teacher_w, student_w, teacher_t, student_t):
    blocks = (CH, 2, NX, 2, OWN, CW)
    dma = pltpu.SemaphoreType.DMA
    scratch = [
        pltpu.VMEM((CH, SEQ, CW), BF),
        pltpu.VMEM((CH, SEQ, CW), BF),
        pltpu.VMEM((2,) + teacher_t.shape, BF),
        pltpu.VMEM((2, IMAGES, ROWS, 4 * HD), BF),
        pltpu.VMEM(blocks, F32),
        pltpu.VMEM(blocks, BF),
        pltpu.VMEM((2, NX, 2, OWN, HD), F32),
        pltpu.VMEM((8, CW), F32),
        pltpu.VMEM((8, HD), F32),
        pltpu.VMEM((SEQ, 3 * HD), F32),
        pltpu.VMEM((SEQ, 3 * HD), BF),
        pltpu.VMEM((SEQ, SEQ), F32),
        pltpu.VMEM((SEQ, SEQ), BF),
        pltpu.VMEM((SEQ, HD), F32),
        pltpu.VMEM((SEQ, HD), BF),
        pltpu.VMEM(blocks, BF),
        pltpu.VMEM(blocks, BF),
        pltpu.VMEM(blocks, BF),
        pltpu.VMEM((3, CH, 2, NX, OWN, CW), BF),
        pltpu.VMEM((3, CH, 2, NX, OWN, CW), BF),
        pltpu.VMEM((3, CH, NX - 1, 2, OWN, CW), BF),
        pltpu.VMEM((3, CH, 2, OWN, CW), BF),
        pltpu.VMEM((3, CH, 2, OWN, CW), BF),
        pltpu.VMEM(blocks, BF),
        pltpu.VMEM(blocks, BF),
        pltpu.VMEM(blocks, BF),
        pltpu.VMEM((NY, NZ, ROWS, 4 * HD), BF),
        pltpu.VMEM((2, NZ, HALF, 4 * HD), BF),
        pltpu.VMEM((2, NZ, ROWS, 4 * HD), BF),
        pltpu.VMEM((2, NZ, ROWS, 4 * HD), BF),
        dma((2 * CH + 4,)),
        dma((2, NZ, 2)),
        dma((2, NZ)),
        dma((2, NZ, 2)),
        dma((2, NZ, 2)),
        dma((2, NZ, 2)),
        dma((2, NZ, 2)),
        dma((3, CH)),
        dma((3, CH)),
        dma((3, CH, NX - 1)),
        dma((3, CH, NX - 1)),
        dma((3, CH)),
        dma((3, CH)),
        dma((2, CH, NX - 1)),
        dma((2, CH, NX - 1)),
        dma((2, CH, NX)),
        dma((2, CH, NX)),
        dma((2, NZ)),
        dma((2, NZ)),
        dma((2, NZ)),
        dma((2, NZ)),
        dma((NZ,)),
        dma((2, NZ)),
    ]
    out_v, out_g = pl.pallas_call(
        kernel,
        name="distill_step",
        out_shape=(jax.ShapeDtypeStruct((OWN, D), BF), jax.ShapeDtypeStruct((ROWS, 4 * HD), BF)),
        in_specs=[pl.BlockSpec(memory_space=pltpu.SMEM)] + [pl.BlockSpec(memory_space=pl.ANY)] * 6,
        out_specs=(pl.BlockSpec(memory_space=pltpu.VMEM), pl.BlockSpec(memory_space=pltpu.VMEM)),
        scratch_shapes=scratch,
        compiler_params=pltpu.CompilerParams(
            collective_id=0, has_side_effects=True, vmem_limit_bytes=60 * 1024 * 1024
        ),
        cost_estimate=pl.CostEstimate(flops=4_000_000_000, bytes_accessed=4_000_000, transcendentals=200_000),
    )(time_index, clean[0], noise[0], teacher_w, student_w, teacher_t, student_t)
    return (out_v[None], out_g)


def solution(mesh):
    placed = (
        P("dp", None, None),
        P("dp", None, None),
        P("dp"),
        P("dp", "tp"),
        P("dp", "tp"),
        P(None, "tp"),
        P(None, "tp"),
    )
    return jax.shard_map(
        on_device,
        mesh=mesh,
        in_specs=placed,
        out_specs=(P("dp", "tp", None), P("dp", "tp")),
        check_vma=False,
    )
```

```python
import functools
import math

import jax
import jax.numpy as jnp
from jax import lax
from jax.experimental import pallas as pl
from jax.experimental.pallas import tpu as pltpu
from jax.sharding import PartitionSpec as P

D = 3072
HD = 128
STEPS = 1000
IMAGES = 32
NY, NZ, NX = 4, 8, 4
NG = NZ // 2
CH = 4
CW = D // CH
ROWS = D // IMAGES
HALF = ROWS // 2
SEQ = 256
OWN = 16
BF = jnp.bfloat16
F32 = jnp.float32
MESH = pl.DeviceIdType.MESH


def mm(a, b):
    return jnp.dot(a, b, preferred_element_type=F32)


def mm_t(a, b):
    return lax.dot_general(a, b, (((1,), (1,)), ((), ())), preferred_element_type=F32)


def t_mm(a, b):
    return lax.dot_general(a, b, (((0,), (0,)), ((), ())), preferred_element_type=F32)


def kernel(
    time_ref,
    clean_hbm,
    noise_hbm,
    wt_hbm,
    ws_hbm,
    tt_hbm,
    ts_hbm,
    out_v,
    out_g,
    clean,
    noise,
    tables,
    w,
    noisy,
    normed,
    inv,
    trig,
    gates,
    acc,
    proj,
    att,
    att_b,
    attended,
    gated,
    term,
    s_term,
    g_term,
    core_in,
    x_sum,
    x_in,
    z_sum,
    z_in,
    vel,
    gap,
    grad,
    y_half,
    y_full,
    z_flow,
    load_sem,
    wz_s,
    wz_r,
    wy_s,
    wy_r,
    wh_s,
    wh_r,
    c_s,
    c_r,
    x_s,
    x_r,
    z_s,
    z_r,
    ax_s,
    ax_r,
    ac_s,
    ac_r,
    gh_s,
    gh_r,
    gf_s,
    gf_r,
    gz_s,
    gz_r,
):
    dp, tp = lax.axis_index("dp"), lax.axis_index("tp")
    y, zl = dp // NZ, dp % NZ
    zh, x, c = tp // (2 * NX), (tp // 2) % NX, tp % 2

    def at(yy, zz, hh, xx, cc):
        return (yy * NZ + zz, hh * 2 * NX + xx * 2 + cc)

    def y_to(k):
        return at((y + k + NY) % NY, zl, zh, x, c)

    def z_to(k):
        return at(y, (zl + k + NZ) % NZ, zh, x, c)

    def x_to(k):
        return at(y, zl, zh, (x + k + NX) % NX, c)

    core_dev = at(y, zl, zh, x, 1 - c)
    far_dev = at(y, zl, 1 - zh, x, c)

    def rcopy(src, dst, send, recv, device):
        return pltpu.make_async_remote_copy(
            src_ref=src, dst_ref=dst, send_sem=send, recv_sem=recv, device_id=device, device_id_type=MESH
        )

    loads = []
    n_load = 0
    for j in range(CH):
        for src, dst in ((clean_hbm, clean), (noise_hbm, noise)):
            loads.append(
                pltpu.make_async_copy(src.at[:, pl.ds(j * CW, CW)], dst.at[j], load_sem.at[n_load])
            )
            n_load += 1
    for m, src in enumerate((tt_hbm, ts_hbm)):
        loads.append(pltpu.make_async_copy(src, tables.at[m], load_sem.at[n_load]))
        n_load += 1
    w_hbm = (wt_hbm, ws_hbm)
    own_w = []
    for m in range(2):
        own_w.append(pltpu.make_async_copy(w_hbm[m], w.at[m, dp], load_sem.at[n_load]))
        n_load += 1
    for copy in own_w + loads:
        copy.start()

    barrier = pltpu.get_barrier_semaphore()
    partners = [far_dev, z_to(NG), z_to(1), z_to(-1), x_to(2), y_to(1), y_to(-1), x_to(1), x_to(3), core_dev]
    for device in partners:
        pl.semaphore_signal(barrier, inc=1, device_id=device, device_id_type=MESH)
    pl.semaphore_wait(barrier, len(partners))

    inner_r, inner_l = zl < NZ - 1, zl > 0
    events = [
        (zl, zl >= 0, 3, inner_r, inner_l),
        (zl - 1, zl >= 1, 0, inner_r, None),
        (zl + 1, zl + 1 < NZ, 1, None, inner_l),
        ((zl + NG) % NZ, zl >= 0, 2, inner_r, inner_l),
        (zl - 2, zl >= 2, 0, inner_r & (zl - 2 >= NG), None),
        (zl + 2, zl + 2 < NZ, 1, None, inner_l & (zl + 2 < NG)),
        ((zl + 3) % NZ, inner_l, 0, inner_r & (zl >= 5), None),
        ((zl + 5) % NZ, inner_r, 1, None, inner_l & (zl <= 2)),
        (zl - 3, zl - 3 >= NG, 0, None, None),
        (zl + 3, zl + 3 < NG, 1, None, None),
        (zl - 6, zl >= 6, 0, inner_r, None),
        (zl + 6, zl + 6 < NZ, 1, None, inner_l),
        (zl - 7, zl >= 7, 0, None, None),
        (zl + 7, zl + 7 < NZ, 1, None, None),
    ]

    def wblk(m, yy, o, p):
        return w.at[m, ((yy + NY) % NY) * NZ + o, pl.ds(p * HALF, HALF)]

    def wz_copy(m, o, way, own=False):
        blk = w.at[m, y * NZ + o]
        src = w_hbm[m] if own else blk
        device = z_to((1, -1, NG)[way])
        return rcopy(src, blk, wz_s.at[m, o, way], wz_r.at[m, o], device)

    def when(there):
        return (lambda f: None) if there is None else pl.when(there)

    def wy_copy(m, o, way, p, own=False):
        blk = wblk(m, y, o, p)
        src = w_hbm[m].at[pl.ds(p * HALF, HALF)] if own else blk
        return rcopy(src, blk, wy_s.at[m, o, way, p], wy_r.at[m, o, way, p], y_to(1 - 2 * way))

    def wy_arrival(m, o, way, p):
        blk = wblk(m, y - 1 + 2 * way, o, p)
        return rcopy(blk, blk, wy_s.at[m, o, way, p], wy_r.at[m, o, way, p], y_to(1 - 2 * way))

    def wh_copy(m, o, way):
        blk = wblk(m, y - 1 + 2 * way, o, way)
        return rcopy(blk, blk, wh_s.at[m, o, way], wh_r.at[m, o, way], y_to(1 - 2 * way))

    def wh_arrival(m, o, way):
        blk = wblk(m, y + 2, o, way)
        return rcopy(blk, blk, wh_s.at[m, o, way], wh_r.at[m, o, way], y_to(1 - 2 * way))

    def wy_start(m, o, own=False):
        for p in range(2):
            for way in range(2):
                wy_copy(m, o, way, (p + way) % 2, own).start()

    def w_zstep(m, e, with_y=True):
        o, there, side, right, left = events[e]

        @pl.when(there)
        def _():
            if e:
                wz_copy(m, o, 0).wait_recv()
            else:
                wz_copy(m, o, 2, True).start()

            @when(right)
            def _():
                wz_copy(m, o, 0, e == 0).start()

            @when(left)
            def _():
                wz_copy(m, o, 1, e == 0).start()

            if with_y:
                wy_start(m, o, e == 0)

    def wy_later(m, e):
        @pl.when(events[e][1])
        def _():
            wy_start(m, events[e][0], e == 0)

    def w_ystep(m, e):
        o, there = events[e][:2]

        @pl.when(there)
        def _():
            for way in range(2):
                wy_arrival(m, o, way, way).wait_recv()
                wh_copy(m, o, way).start()

    def w_hwait(m):
        def body(o, carry):
            for way in range(2):
                wy_arrival(m, o, way, 1 - way).wait_recv()
                wh_arrival(m, o, way).wait_recv()
            return carry

        lax.fori_loop(0, NZ, body, 0)
        own_w[m].wait()

    def w_drain(m):
        wz_copy(m, zl, 2).wait_send()
        for o, there, side, right, left in events:
            for way, onward in ((0, right), (1, left)):
                if onward is not None:

                    @pl.when(there & onward)
                    def _():
                        wz_copy(m, o, way).wait_send()

        def body(o, carry):
            for way in range(2):
                for p in range(2):
                    wy_copy(m, o, way, p).wait_send()
                wh_copy(m, o, way).wait_send()
            return carry

        lax.fori_loop(0, NZ, body, 0)

    def cs_copy(n, buf, j):
        return rcopy(buf.at[j, :, :, 1 - c], core_in.at[n, j], c_s.at[n, j], c_r.at[n, j], core_dev)

    def xs_copy(n, j, k):
        return rcopy(
            x_sum.at[n, j, :, (x + k) % NX], x_in.at[n, j, k - 1], x_s.at[n, j, k - 1], x_r.at[n, j, k - 1], x_to(k)
        )

    def zs_copy(n, j):
        if n == 2:
            return rcopy(z_sum.at[n, j, 1 - zh], z_in.at[n, j, zh], z_s.at[n, j], z_r.at[n, j], far_dev)
        return rcopy(z_sum.at[n, j], z_in.at[n, j], z_s.at[n, j], z_r.at[n, j], far_dev)

    def zs_arrival(n, j):
        if n == 2:
            return rcopy(z_sum.at[n, j, zh], z_in.at[n, j, 1 - zh], z_s.at[n, j], z_r.at[n, j], far_dev)
        return zs_copy(n, j)

    def ax_copy(n, buf, j, k):
        mine = buf.at[j, :, x, c]
        return rcopy(mine, mine, ax_s.at[n, j, k - 1], ax_r.at[n, j, k - 1], x_to(k))

    def ax_arrival(n, buf, j, k):
        blk = buf.at[j, :, (x + NX - k) % NX, c]
        return rcopy(blk, blk, ax_s.at[n, j, k - 1], ax_r.at[n, j, k - 1], x_to(k))

    def ac_copy(n, buf, j, k, cc):
        blk = buf.at[j, :, (x + NX - k) % NX, cc]
        return rcopy(blk, blk, ac_s.at[n, j, k], ac_r.at[n, j, k], core_dev)

    def sum_x_start(n, buf, j):
        cs_copy(n, buf, j).wait_recv()
        for hh in range(2):
            for xx in range(NX):
                total = buf[j, hh, xx, c].astype(F32) + core_in[n, j, hh, xx].astype(F32)
                x_sum[n, j, hh, xx] = total.astype(BF)
        for k in (2, 1, 3):
            xs_copy(n, j, k).start()

    def sum_z_start(n, j):
        for k in range(1, NX):
            xs_copy(n, j, k).wait_recv()
        for hh in range(2):
            total = x_sum[n, j, hh, x].astype(F32)
            for k in range(NX - 1):
                total = total + x_in[n, j, k, hh].astype(F32)
            z_sum[n, j, hh] = total.astype(BF)
        zs_copy(n, j).start()

    def share_start(n, buf, j):
        for k in (2, 1, 3):
            ax_copy(n, buf, j, k).start()
        ac_copy(n, buf, j, 0, c).start()

    def share_forward(n, buf, j):
        for k in (1, 3, 2):
            ax_arrival(n, buf, j, k).wait_recv()
            ac_copy(n, buf, j, k, c).start()

    def share_wait(n, buf, j):
        for k in range(NX):
            ac_copy(n, buf, j, k, 1 - c).wait_recv()

    def sum_drain(n, buf, shared):
        for j in range(CH):
            cs_copy(n, buf, j).wait_send()
            for k in range(1, NX):
                xs_copy(n, j, k).wait_send()
            zs_copy(n, j).wait_send()
            if shared is not None:
                for k in range(1, NX):
                    ax_copy(n, shared, j, k).wait_send()
                for k in range(NX):
                    ac_copy(n, shared, j, k, c).wait_send()

    def project(src, m):
        acc[...] = jnp.zeros_like(acc)

        @pl.loop(0, CH)
        def _(j):
            left = src[j].reshape(SEQ, CW)
            right = w[m, pl.ds(NZ * j, NZ), :, 0 : 3 * HD].reshape(CW, 3 * HD)
            acc[...] += mm(left, right)

        return acc[...].astype(BF)

    scale = HD ** (-0.5)

    def attend(m):
        queries, keys, values = (proj[:, i * HD : (i + 1) * HD] for i in range(3))
        scores = mm_t(queries, keys) * scale
        top = jnp.max(scores, axis=-1, keepdims=True)
        raised = jnp.exp(scores - top)
        probs = raised / jnp.sum(raised, axis=-1, keepdims=True)
        att[...] = probs
        att_b[...] = probs.astype(BF)
        attended[...] = mm(att_b[...], values)
        gated[...] = (attended[...] * (1.0 + gates[pl.ds(m, 1)])).astype(BF)

    def out_columns(m, j):
        return w[m, pl.ds(NZ * j, NZ), :, 3 * HD :].reshape(CW, HD)

    shape6 = (2, NX, 2, OWN, CW)

    w_zstep(0, 0)

    for e in range(1, 4):
        w_zstep(0, e)
    for copy in loads[2 * CH :]:
        copy.wait()
    steps = jnp.full((1, CW), time_ref[0].astype(F32))
    step_time = 0.05 + 1.45 * (steps + 0.5) / STEPS
    trig[pl.ds(0, 1)] = jnp.cos(step_time)
    trig[pl.ds(1, 1)] = jnp.sin(step_time)

    half = tables.shape[1] // 2
    position = lax.broadcasted_iota(jnp.int32, (half, HD), 0).astype(F32)
    frequency = 4.0 * jnp.exp(-math.log(100.0) * position / half)
    phases = step_time[:, :HD] * frequency
    cos_p, sin_p = jnp.cos(phases), jnp.sin(phases)
    for m in range(2):
        low, high = tables[m, :half].astype(F32), tables[m, half:].astype(F32)
        gates[pl.ds(m, 1)] = jnp.sum(cos_p * low + sin_p * high, axis=0, keepdims=True)
        if m == 1:
            gates[pl.ds(2, 1)] = jnp.sum(frequency * (cos_p * high - sin_p * low), axis=0, keepdims=True)

    for e in range(4, 8):
        w_zstep(0, e)
    for e in (0, 1, 2):
        w_ystep(0, e)
    for copy in loads[: 2 * CH]:
        copy.wait()

    def mix(r):
        hh, xx, cc = r // (2 * NX), (r // 2) % NX, r % 2
        cosine, sine = trig[pl.ds(0, 1)], trig[pl.ds(1, 1)]
        square = jnp.zeros((OWN, 1), F32)
        for j in range(CH):
            rows = pl.ds(pl.multiple_of(r * OWN, OWN), OWN)
            mixed = cosine * clean[j, rows].astype(F32) + sine * noise[j, rows].astype(F32)
            noisy[j, hh, xx, cc] = mixed
            square = square + jnp.sum(mixed * mixed, axis=-1, keepdims=True)
        factor = lax.rsqrt(square / D + 1e-06)
        inv[hh, xx, cc] = jnp.broadcast_to(factor, (OWN, HD))
        for j in range(CH):
            normed[j, hh, xx, cc] = (noisy[j, hh, xx, cc] * factor).astype(BF)

    def mix_rows(first, end):
        pl.loop(first, end)(mix)

    mix_rows(0, 6)
    for e in range(8, 12):
        w_zstep(0, e)
    for e in (3, 4, 5):
        w_ystep(0, e)
    mix_rows(6, 11)
    for e in (12, 13):
        w_zstep(0, e)
    w_zstep(1, 0, False)
    mix_rows(11, 16)
    for e in (6, 7, 8, 9, 10, 11, 12, 13):
        w_ystep(0, e)
    w_hwait(0)
    wy_later(1, 0)
    for e in (1, 2, 3):
        w_zstep(1, e)

    proj[...] = project(normed, 0)
    attend(0)
    for j in range(CH):
        term[j] = mm_t(gated[...], out_columns(0, j)).astype(BF).reshape(shape6)
        cs_copy(0, term, j).start()
    for e in (4, 5, 6, 7):
        w_zstep(1, e)

    def velocity_rows(j):
        zs_arrival(0, j).wait_recv()
        for hh in range(2):
            total = z_sum[0, j, hh].astype(F32) + z_in[0, j, hh].astype(F32)
            vel[j, hh, x, c] = (noisy[j, hh, x, c] + total).astype(BF)
        share_start(0, vel, j)

    for j in range(CH):
        sum_x_start(0, term, j)
    for e in (8, 9, 10, 11):
        w_zstep(1, e)
    for j in range(CH):
        sum_z_start(0, j)
    for e in (12, 13):
        w_zstep(1, e)
    for e in (0, 1, 2, 3, 4, 5, 6, 7):
        w_ystep(1, e)
    velocity_rows(0)
    for e in (8, 9, 10, 11):
        w_ystep(1, e)
    velocity_rows(1)
    share_forward(0, vel, 0)
    for e in (12, 13):
        w_ystep(1, e)
    velocity_rows(2)
    share_forward(0, vel, 1)
    velocity_rows(3)
    share_forward(0, vel, 2)
    w_hwait(1)
    proj[...] = project(normed, 1)

    attend(1)
    share_forward(0, vel, 3)
    for j in range(CH):
        s_term[j] = mm_t(gated[...], out_columns(1, j)).astype(BF).reshape(shape6)

    moved = jnp.zeros((SEQ, 3 * HD), F32)
    inner = jnp.zeros((SEQ, 1), F32)
    for j in range(CH):
        share_wait(0, vel, j)
        arrived = vel[j].reshape(SEQ, CW)
        product = noisy[j].reshape(SEQ, CW) * arrived.astype(F32)
        inner = inner + jnp.sum(product, axis=-1, keepdims=True)
        moved = moved + mm(arrived, w[1, NZ * j : NZ * (j + 1), :, 0 : 3 * HD].reshape(CW, 3 * HD))
    factor = inv[...].reshape(SEQ, HD)[:, :1]
    d_proj = (factor * (moved - factor * inner / D * acc[...])).astype(BF)
    d_queries, d_keys, d_values = (d_proj[:, i * HD : (i + 1) * HD] for i in range(3))
    d_scores = (mm_t(d_queries, proj[:, HD : 2 * HD]) + mm_t(proj[:, :HD], d_keys)) * scale
    probs = att[...]
    d_probs = probs * (d_scores - jnp.sum(probs * d_scores, axis=-1, keepdims=True))
    d_attended = mm(d_probs.astype(BF), proj[:, 2 * HD :]) + mm(att_b[...], d_values)
    d_gated = (d_attended * (1.0 + gates[1:2]) + attended[...] * gates[2:3]).astype(BF)
    for j in range(CH):
        d_term = mm_t(d_gated, out_columns(1, j)).astype(BF).astype(F32)
        cosine, sine = trig[0:1], trig[1:2]
        both = cosine * cosine * s_term[j].reshape(SEQ, CW).astype(F32) + cosine * sine * d_term
        g_term[j] = both.astype(BF).reshape(shape6)
        cs_copy(1, g_term, j).start()

    def gap_rows(j):
        zs_arrival(1, j).wait_recv()
        cosine, sine = trig[0:1], trig[1:2]
        for hh in range(2):
            total = z_sum[1, j, hh].astype(F32) + z_in[1, j, hh].astype(F32)
            clear = -(cosine * cosine + cosine * sine) * noisy[j, hh, x, c]
            moved = (cosine * cosine - cosine * sine) * vel[j, hh, x, c].astype(F32)
            gap[j, hh, x, c] = (clear + moved - total).astype(BF)
        share_start(1, gap, j)

    for j in range(CH):
        sum_x_start(1, g_term, j)
    for j in range(CH):
        cs_copy(2, s_term, j).start()
    for j in range(CH):
        sum_z_start(1, j)
    for j in range(CH):
        sum_x_start(2, s_term, j)
    gap_rows(0)
    gap_rows(1)
    share_forward(1, gap, 0)
    sum_z_start(2, 0)
    sum_z_start(2, 1)
    gap_rows(2)
    share_forward(1, gap, 1)
    sum_z_start(2, 2)
    sum_z_start(2, 3)
    gap_rows(3)
    share_forward(1, gap, 2)
    share_forward(1, gap, 3)

    square = jnp.zeros((1, 1), F32)
    back = jnp.zeros((SEQ, HD), F32)
    for j in range(CH):
        share_wait(1, gap, j)
        whole = gap[j].reshape(SEQ, CW)
        wide = whole.astype(F32)
        rows = jnp.sum(wide * wide, axis=0, keepdims=True)
        square = square + jnp.sum(rows, axis=1, keepdims=True)
        back = back + mm(whole, out_columns(1, j))
    cot = -math.sqrt(D / IMAGES) / (jnp.sqrt(square) + 0.1)
    d_att_b = (back * cot * (1.0 + gates[1:2])).astype(BF)
    queries, keys, values = (proj[:, i * HD : (i + 1) * HD] for i in range(3))
    grad_values = t_mm(att_b[...], d_att_b)
    d_back = mm_t(d_att_b, values)
    probs = att[...]
    d_scores_b = (probs * (d_back - jnp.sum(probs * d_back, axis=-1, keepdims=True)) * scale).astype(BF)
    grad_queries = mm(d_scores_b, keys)
    grad_keys = t_mm(d_scores_b, queries)
    d_proj_b = jnp.concatenate([grad_queries, grad_keys, grad_values], axis=1).astype(BF)

    def gh_copy(d, way):
        part = pl.ds(way * HALF, HALF)
        return rcopy(
            grad.at[(y + 2) % NY, d, part], y_half.at[way, d], gh_s.at[way, d], gh_r.at[way, d], y_to(1 - 2 * way)
        )

    def gf_copy(d, way):
        return rcopy(
            grad.at[(y + 1 - 2 * way + NY) % NY, d],
            y_full.at[way, d],
            gf_s.at[way, d],
            gf_r.at[way, d],
            y_to(1 - 2 * way),
        )

    def gz_copy(d, way):
        dst = z_flow.at[2, 0] if way == 2 else z_flow.at[way, d]
        recv = gz_r.at[2, 0] if way == 2 else gz_r.at[way, d]
        return rcopy(grad.at[y, d], dst, gz_s.at[d], recv, z_to((-1, 1, NG)[way]))

    late_first = (12, 13, 10, 11, 6, 7, 8, 9, 3, 4, 5, 1, 2, 0)

    for k in (2, 1, 3, 0):
        yy = (y + k) % NY
        left = t_mm(normed[yy].reshape(SEQ, CW), d_proj_b)
        grad[yy, :, :, 0 : 3 * HD] = left.astype(BF).reshape(NZ, ROWS, 3 * HD)
        right = t_mm(gap[yy].reshape(SEQ, CW), gated[...]) * cot
        grad[yy, :, :, 3 * HD :] = right.astype(BF).reshape(NZ, ROWS, HD)
        if k == 2:

            for e in late_first:

                @pl.when(events[e][1])
                def _():
                    for way in range(2):
                        gh_copy(events[e][0], way).start()

    def y_second(d):
        for way in range(2):
            gh_copy(d, way).wait_recv()
            yy = (y + 1 - 2 * way + NY) % NY
            part = pl.ds(way * HALF, HALF)
            total = grad[yy, d, part].astype(F32) + y_half[way, d].astype(F32)
            grad[yy, d, part] = total.astype(BF)
            gf_copy(d, way).start()

    for e in late_first:

        @pl.when(events[e][1])
        def _():
            y_second(events[e][0])

    for e in late_first:
        d, there, side, right, left = events[e]

        @pl.when(there)
        def _():
            for way in range(2):
                gf_copy(d, way).wait_recv()
            grad[y, d] = (grad[y, d].astype(F32) + y_full[0, d].astype(F32) + y_full[1, d].astype(F32)).astype(BF)
            for way, child in ((0, right), (1, left)):

                @when(child)
                def _():
                    gz_copy(d, way).wait_recv()
                    grad[y, d] = (grad[y, d].astype(F32) + z_flow[way, d].astype(F32)).astype(BF)

            if e:
                gz_copy(d, side).start()
            else:
                gz_copy(d, 2).wait_recv()
                out_g[...] = (grad[y, d].astype(F32) + z_flow[2, 0].astype(F32)).astype(BF)

    for j in range(CH):
        zs_arrival(2, j).wait_recv()
        total = z_sum[2, j, zh].astype(F32) + z_in[2, j, 1 - zh].astype(F32)
        out_v[:, j * CW : (j + 1) * CW] = (noisy[j, zh, x, c] + total).astype(BF)

    w_drain(0)
    w_drain(1)
    sum_drain(0, term, vel)
    sum_drain(1, g_term, gap)
    sum_drain(2, s_term, None)

    @pl.loop(0, NZ)
    def _(d):
        for way in range(2):
            gh_copy(d, way).wait_send()
            gf_copy(d, way).wait_send()

        @pl.when(d != zl)
        def _():
            gz_copy(d, 0).wait_send()


def on_device(clean, noise, time_index, teacher_w, student_w, teacher_t, student_t):
    blocks = (CH, 2, NX, 2, OWN, CW)
    dma = pltpu.SemaphoreType.DMA
    scratch = [
        pltpu.VMEM((CH, SEQ, CW), BF),
        pltpu.VMEM((CH, SEQ, CW), BF),
        pltpu.VMEM((2,) + teacher_t.shape, BF),
        pltpu.VMEM((2, IMAGES, ROWS, 4 * HD), BF),
        pltpu.VMEM(blocks, F32),
        pltpu.VMEM(blocks, BF),
        pltpu.VMEM((2, NX, 2, OWN, HD), F32),
        pltpu.VMEM((8, CW), F32),
        pltpu.VMEM((8, HD), F32),
        pltpu.VMEM((SEQ, 3 * HD), F32),
        pltpu.VMEM((SEQ, 3 * HD), BF),
        pltpu.VMEM((SEQ, SEQ), F32),
        pltpu.VMEM((SEQ, SEQ), BF),
        pltpu.VMEM((SEQ, HD), F32),
        pltpu.VMEM((SEQ, HD), BF),
        pltpu.VMEM(blocks, BF),
        pltpu.VMEM(blocks, BF),
        pltpu.VMEM(blocks, BF),
        pltpu.VMEM((3, CH, 2, NX, OWN, CW), BF),
        pltpu.VMEM((3, CH, 2, NX, OWN, CW), BF),
        pltpu.VMEM((3, CH, NX - 1, 2, OWN, CW), BF),
        pltpu.VMEM((3, CH, 2, OWN, CW), BF),
        pltpu.VMEM((3, CH, 2, OWN, CW), BF),
        pltpu.VMEM(blocks, BF),
        pltpu.VMEM(blocks, BF),
        pltpu.VMEM((NY, NZ, ROWS, 4 * HD), BF),
        pltpu.VMEM((2, NZ, HALF, 4 * HD), BF),
        pltpu.VMEM((2, NZ, ROWS, 4 * HD), BF),
        pltpu.VMEM((3, NZ, ROWS, 4 * HD), BF),
        dma((2 * CH + 4,)),
        dma((2, NZ, 3)),
        dma((2, NZ)),
        dma((2, NZ, 2, 2)),
        dma((2, NZ, 2, 2)),
        dma((2, NZ, 2)),
        dma((2, NZ, 2)),
        dma((3, CH)),
        dma((3, CH)),
        dma((3, CH, NX - 1)),
        dma((3, CH, NX - 1)),
        dma((3, CH)),
        dma((3, CH)),
        dma((2, CH, NX - 1)),
        dma((2, CH, NX - 1)),
        dma((2, CH, NX)),
        dma((2, CH, NX)),
        dma((2, NZ)),
        dma((2, NZ)),
        dma((2, NZ)),
        dma((2, NZ)),
        dma((NZ,)),
        dma((3, NZ)),
    ]
    out_v, out_g = pl.pallas_call(
        kernel,
        name="distill_step",
        out_shape=(jax.ShapeDtypeStruct((OWN, D), BF), jax.ShapeDtypeStruct((ROWS, 4 * HD), BF)),
        in_specs=[pl.BlockSpec(memory_space=pltpu.SMEM)] + [pl.BlockSpec(memory_space=pl.ANY)] * 6,
        out_specs=(pl.BlockSpec(memory_space=pltpu.VMEM), pl.BlockSpec(memory_space=pltpu.VMEM)),
        scratch_shapes=scratch,
        compiler_params=pltpu.CompilerParams(
            collective_id=0, has_side_effects=True, vmem_limit_bytes=60 * 1024 * 1024
        ),
        cost_estimate=pl.CostEstimate(flops=4_000_000_000, bytes_accessed=4_000_000, transcendentals=200_000),
    )(time_index, clean[0], noise[0], teacher_w, student_w, teacher_t, student_t)
    return (out_v[None], out_g)


def solution(mesh):
    placed = (
        P("dp", None, None),
        P("dp", None, None),
        P("dp"),
        P("dp", "tp"),
        P("dp", "tp"),
        P(None, "tp"),
        P(None, "tp"),
    )
    return jax.shard_map(
        on_device,
        mesh=mesh,
        in_specs=placed,
        out_specs=(P("dp", "tp", None), P("dp", "tp")),
        check_vma=False,
    )
```

```python
import functools
import math

import jax
import jax.numpy as jnp
from jax import lax
from jax.experimental import pallas as pl
from jax.experimental.pallas import tpu as pltpu
from jax.sharding import PartitionSpec as P

D = 3072
HD = 128
STEPS = 1000
IMAGES = 32
NY, NZ, NX = 4, 8, 4
NG = NZ // 2
CH = 4
CW = D // CH
ROWS = D // IMAGES
HALF = ROWS // 2
SEQ = 256
OWN = 16
BF = jnp.bfloat16
F32 = jnp.float32
MESH = pl.DeviceIdType.MESH


def mm(a, b):
    return jnp.dot(a, b, preferred_element_type=F32)


def mm_t(a, b):
    return lax.dot_general(a, b, (((1,), (1,)), ((), ())), preferred_element_type=F32)


def t_mm(a, b):
    return lax.dot_general(a, b, (((0,), (0,)), ((), ())), preferred_element_type=F32)


def kernel(
    time_ref,
    clean_hbm,
    noise_hbm,
    wt_hbm,
    ws_hbm,
    tt_hbm,
    ts_hbm,
    out_v,
    out_g,
    clean,
    noise,
    tables,
    w,
    noisy,
    normed,
    inv,
    trig,
    gates,
    acc,
    proj,
    att,
    att_b,
    attended,
    gated,
    term,
    s_term,
    g_term,
    core_in,
    x_sum,
    x_in,
    z_sum,
    z_in,
    vel,
    gap,
    grad,
    y_half,
    y_full,
    z_flow,
    load_sem,
    wz_s,
    wz_r,
    wy_s,
    wy_r,
    wh_s,
    wh_r,
    c_s,
    c_r,
    x_s,
    x_r,
    z_s,
    z_r,
    ax_s,
    ax_r,
    ac_s,
    ac_r,
    gh_s,
    gh_r,
    gf_s,
    gf_r,
    gz_s,
    gz_r,
):
    dp, tp = lax.axis_index("dp"), lax.axis_index("tp")
    y, zl = dp // NZ, dp % NZ
    zh, x, c = tp // (2 * NX), (tp // 2) % NX, tp % 2

    def at(yy, zz, hh, xx, cc):
        return (yy * NZ + zz, hh * 2 * NX + xx * 2 + cc)

    def y_to(k):
        return at((y + k + NY) % NY, zl, zh, x, c)

    def z_to(k):
        return at(y, (zl + k + NZ) % NZ, zh, x, c)

    def x_to(k):
        return at(y, zl, zh, (x + k + NX) % NX, c)

    core_dev = at(y, zl, zh, x, 1 - c)
    far_dev = at(y, zl, 1 - zh, x, c)

    def rcopy(src, dst, send, recv, device):
        return pltpu.make_async_remote_copy(
            src_ref=src, dst_ref=dst, send_sem=send, recv_sem=recv, device_id=device, device_id_type=MESH
        )

    loads = []
    n_load = 0
    for j in range(CH):
        for src, dst in ((clean_hbm, clean), (noise_hbm, noise)):
            loads.append(
                pltpu.make_async_copy(src.at[:, pl.ds(j * CW, CW)], dst.at[j], load_sem.at[n_load])
            )
            n_load += 1
    for m, src in enumerate((tt_hbm, ts_hbm)):
        loads.append(pltpu.make_async_copy(src, tables.at[m], load_sem.at[n_load]))
        n_load += 1
    w_hbm = (wt_hbm, ws_hbm)
    own_w = []
    for m in range(2):
        own_w.append(pltpu.make_async_copy(w_hbm[m], w.at[m, dp], load_sem.at[n_load]))
        n_load += 1
    for copy in own_w + loads:
        copy.start()

    barrier = pltpu.get_barrier_semaphore()
    partners = [far_dev, z_to(NG), z_to(1), z_to(-1), x_to(2), y_to(1), y_to(-1), x_to(1), x_to(3), core_dev]
    for device in partners:
        pl.semaphore_signal(barrier, inc=1, device_id=device, device_id_type=MESH)

    inner_r, inner_l = zl < NZ - 1, zl > 0
    events = [
        (zl, zl >= 0, 3, inner_r, inner_l),
        (zl - 1, zl >= 1, 0, inner_r, None),
        (zl + 1, zl + 1 < NZ, 1, None, inner_l),
        ((zl + NG) % NZ, zl >= 0, 2, inner_r, inner_l),
        (zl - 2, zl >= 2, 0, inner_r & (zl - 2 >= NG), None),
        (zl + 2, zl + 2 < NZ, 1, None, inner_l & (zl + 2 < NG)),
        ((zl + 3) % NZ, inner_l, 0, inner_r & (zl >= 5), None),
        ((zl + 5) % NZ, inner_r, 1, None, inner_l & (zl <= 2)),
        (zl - 3, zl - 3 >= NG, 0, None, None),
        (zl + 3, zl + 3 < NG, 1, None, None),
        (zl - 6, zl >= 6, 0, inner_r, None),
        (zl + 6, zl + 6 < NZ, 1, None, inner_l),
        (zl - 7, zl >= 7, 0, None, None),
        (zl + 7, zl + 7 < NZ, 1, None, None),
    ]

    def wblk(m, yy, o, p):
        return w.at[m, ((yy + NY) % NY) * NZ + o, pl.ds(p * HALF, HALF)]

    def wz_copy(m, o, way, own=False):
        blk = w.at[m, y * NZ + o]
        src = w_hbm[m] if own else blk
        device = z_to((1, -1, NG)[way])
        return rcopy(src, blk, wz_s.at[m, o, way], wz_r.at[m, o], device)

    def when(there):
        return (lambda f: None) if there is None else pl.when(there)

    def wy_copy(m, o, way, p, own=False):
        blk = wblk(m, y, o, p)
        src = w_hbm[m].at[pl.ds(p * HALF, HALF)] if own else blk
        return rcopy(src, blk, wy_s.at[m, o, way, p], wy_r.at[m, o, way, p], y_to(1 - 2 * way))

    def wy_arrival(m, o, way, p):
        blk = wblk(m, y - 1 + 2 * way, o, p)
        return rcopy(blk, blk, wy_s.at[m, o, way, p], wy_r.at[m, o, way, p], y_to(1 - 2 * way))

    def wh_copy(m, o, way):
        blk = wblk(m, y - 1 + 2 * way, o, way)
        return rcopy(blk, blk, wh_s.at[m, o, way], wh_r.at[m, o, way], y_to(1 - 2 * way))

    def wh_arrival(m, o, way):
        blk = wblk(m, y + 2, o, way)
        return rcopy(blk, blk, wh_s.at[m, o, way], wh_r.at[m, o, way], y_to(1 - 2 * way))

    def wy_start(m, o, own=False):
        for p in range(2):
            for way in range(2):
                wy_copy(m, o, way, (p + way) % 2, own).start()

    def w_zstep(m, e, with_y=True):
        o, there, side, right, left = events[e]

        @pl.when(there)
        def _():
            if e:
                wz_copy(m, o, 0).wait_recv()
            else:
                wz_copy(m, o, 2, True).start()

            @when(right)
            def _():
                wz_copy(m, o, 0, e == 0).start()

            @when(left)
            def _():
                wz_copy(m, o, 1, e == 0).start()

            if with_y:
                wy_start(m, o, e == 0)

    def wy_later(m, e):
        @pl.when(events[e][1])
        def _():
            wy_start(m, events[e][0], e == 0)

    def w_ystep(m, e):
        o, there = events[e][:2]

        @pl.when(there)
        def _():
            for way in range(2):
                wy_arrival(m, o, way, way).wait_recv()
                wh_copy(m, o, way).start()

    def w_near(m):
        def body(o, carry):
            for way in range(2):
                wy_arrival(m, o, way, 1 - way).wait_recv()
            return carry

        lax.fori_loop(0, NZ, body, 0)

    def w_far(m):
        def body(o, carry):
            for way in range(2):
                wh_arrival(m, o, way).wait_recv()
            return carry

        lax.fori_loop(0, NZ, body, 0)

    def w_drain(m):
        wz_copy(m, zl, 2).wait_send()
        for o, there, side, right, left in events:
            for way, onward in ((0, right), (1, left)):
                if onward is not None:

                    @pl.when(there & onward)
                    def _():
                        wz_copy(m, o, way).wait_send()

        def body(o, carry):
            for way in range(2):
                for p in range(2):
                    wy_copy(m, o, way, p).wait_send()
                wh_copy(m, o, way).wait_send()
            return carry

        lax.fori_loop(0, NZ, body, 0)

    def cs_copy(n, buf, j):
        return rcopy(buf.at[j, :, :, 1 - c], core_in.at[n, j], c_s.at[n, j], c_r.at[n, j], core_dev)

    def xs_copy(n, j, k):
        return rcopy(
            x_sum.at[n, j, :, (x + k) % NX], x_in.at[n, j, k - 1], x_s.at[n, j, k - 1], x_r.at[n, j, k - 1], x_to(k)
        )

    def zs_copy(n, j):
        if n == 2:
            return rcopy(z_sum.at[n, j, 1 - zh], z_in.at[n, j, zh], z_s.at[n, j], z_r.at[n, j], far_dev)
        return rcopy(z_sum.at[n, j], z_in.at[n, j], z_s.at[n, j], z_r.at[n, j], far_dev)

    def zs_arrival(n, j):
        if n == 2:
            return rcopy(z_sum.at[n, j, zh], z_in.at[n, j, 1 - zh], z_s.at[n, j], z_r.at[n, j], far_dev)
        return zs_copy(n, j)

    def ax_copy(n, buf, j, k):
        mine = buf.at[j, :, x, c]
        return rcopy(mine, mine, ax_s.at[n, j, k - 1], ax_r.at[n, j, k - 1], x_to(k))

    def ax_arrival(n, buf, j, k):
        blk = buf.at[j, :, (x + NX - k) % NX, c]
        return rcopy(blk, blk, ax_s.at[n, j, k - 1], ax_r.at[n, j, k - 1], x_to(k))

    def ac_copy(n, buf, j, k, cc):
        blk = buf.at[j, :, (x + NX - k) % NX, cc]
        return rcopy(blk, blk, ac_s.at[n, j, k], ac_r.at[n, j, k], core_dev)

    def sum_x_start(n, buf, j):
        cs_copy(n, buf, j).wait_recv()
        for hh in range(2):
            for xx in range(NX):
                total = buf[j, hh, xx, c].astype(F32) + core_in[n, j, hh, xx].astype(F32)
                x_sum[n, j, hh, xx] = total.astype(BF)
        for k in (2, 1, 3):
            xs_copy(n, j, k).start()

    def sum_z_start(n, j):
        for k in range(1, NX):
            xs_copy(n, j, k).wait_recv()
        for hh in range(2):
            total = x_sum[n, j, hh, x].astype(F32)
            for k in range(NX - 1):
                total = total + x_in[n, j, k, hh].astype(F32)
            z_sum[n, j, hh] = total.astype(BF)
        zs_copy(n, j).start()

    def share_start(n, buf, j):
        for k in (2, 1, 3):
            ax_copy(n, buf, j, k).start()
        ac_copy(n, buf, j, 0, c).start()

    def share_forward(n, buf, j):
        for k in (1, 3, 2):
            ax_arrival(n, buf, j, k).wait_recv()
            ac_copy(n, buf, j, k, c).start()

    def share_wait(n, buf, j):
        for k in range(NX):
            ac_copy(n, buf, j, k, 1 - c).wait_recv()

    def sum_drain(n, buf, shared):
        for j in range(CH):
            cs_copy(n, buf, j).wait_send()
            for k in range(1, NX):
                xs_copy(n, j, k).wait_send()
            zs_copy(n, j).wait_send()
            if shared is not None:
                for k in range(1, NX):
                    ax_copy(n, shared, j, k).wait_send()
                for k in range(NX):
                    ac_copy(n, shared, j, k, c).wait_send()

    def project(m, k):
        j = (y + k) % NY
        right = w[m, pl.ds(NZ * j, NZ), :, 0 : 3 * HD].reshape(CW, 3 * HD)
        part = mm(normed[j].reshape(SEQ, CW), right)
        acc[...] = part if k == 0 else acc[...] + part

    def project_rest(m):
        w_near(m)
        project(m, 1)
        project(m, 3)
        w_far(m)
        project(m, 2)
        proj[...] = acc[...].astype(BF)

    scale = HD ** (-0.5)

    def attend(m):
        queries, keys, values = (proj[:, i * HD : (i + 1) * HD] for i in range(3))
        scores = mm_t(queries, keys) * scale
        top = jnp.max(scores, axis=-1, keepdims=True)
        raised = jnp.exp(scores - top)
        probs = raised / jnp.sum(raised, axis=-1, keepdims=True)
        att[...] = probs
        att_b[...] = probs.astype(BF)
        attended[...] = mm(att_b[...], values)
        gated[...] = (attended[...] * (1.0 + gates[pl.ds(m, 1)])).astype(BF)

    def out_columns(m, j):
        return w[m, pl.ds(NZ * j, NZ), :, 3 * HD :].reshape(CW, HD)

    shape6 = (2, NX, 2, OWN, CW)

    for copy in loads[2 * CH :]:
        copy.wait()
    steps = jnp.full((1, CW), time_ref[0].astype(F32))
    step_time = 0.05 + 1.45 * (steps + 0.5) / STEPS
    trig[pl.ds(0, 1)] = jnp.cos(step_time)
    trig[pl.ds(1, 1)] = jnp.sin(step_time)

    half = tables.shape[1] // 2
    position = lax.broadcasted_iota(jnp.int32, (half, HD), 0).astype(F32)
    frequency = 4.0 * jnp.exp(-math.log(100.0) * position / half)
    phases = step_time[:, :HD] * frequency
    cos_p, sin_p = jnp.cos(phases), jnp.sin(phases)
    for m in range(2):
        low, high = tables[m, :half].astype(F32), tables[m, half:].astype(F32)
        gates[pl.ds(m, 1)] = jnp.sum(cos_p * low + sin_p * high, axis=0, keepdims=True)
        if m == 1:
            gates[pl.ds(2, 1)] = jnp.sum(frequency * (cos_p * high - sin_p * low), axis=0, keepdims=True)

    pl.semaphore_wait(barrier, len(partners))
    w_zstep(0, 0)
    for e in range(1, 4):
        w_zstep(0, e)
    for e in range(4, 8):
        w_zstep(0, e)
    for e in (0, 1, 2):
        w_ystep(0, e)
    for copy in loads[: 2 * CH]:
        copy.wait()

    def mix(r):
        hh, xx, cc = r // (2 * NX), (r // 2) % NX, r % 2
        cosine, sine = trig[pl.ds(0, 1)], trig[pl.ds(1, 1)]
        square = jnp.zeros((OWN, 1), F32)
        for j in range(CH):
            rows = pl.ds(pl.multiple_of(r * OWN, OWN), OWN)
            mixed = cosine * clean[j, rows].astype(F32) + sine * noise[j, rows].astype(F32)
            noisy[j, hh, xx, cc] = mixed
            square = square + jnp.sum(mixed * mixed, axis=-1, keepdims=True)
        factor = lax.rsqrt(square / D + 1e-06)
        inv[hh, xx, cc] = jnp.broadcast_to(factor, (OWN, HD))
        for j in range(CH):
            normed[j, hh, xx, cc] = (noisy[j, hh, xx, cc] * factor).astype(BF)

    def mix_rows(first, end):
        pl.loop(first, end)(mix)

    mix_rows(0, 6)
    for e in range(8, 12):
        w_zstep(0, e)
    for e in (3, 4, 5):
        w_ystep(0, e)
    mix_rows(6, 11)
    for e in (12, 13):
        w_zstep(0, e)
    w_zstep(1, 0, False)
    mix_rows(11, 16)
    own_w[0].wait()
    project(0, 0)
    for e in (6, 7, 8, 9, 10, 11, 12, 13):
        w_ystep(0, e)
    project_rest(0)
    wy_later(1, 0)
    for e in (1, 2, 3):
        w_zstep(1, e)

    attend(0)
    for j in range(CH):
        term[j] = mm_t(gated[...], out_columns(0, j)).astype(BF).reshape(shape6)
        cs_copy(0, term, j).start()
    for e in (4, 5, 6, 7):
        w_zstep(1, e)

    def velocity_rows(j):
        zs_arrival(0, j).wait_recv()
        for hh in range(2):
            total = z_sum[0, j, hh].astype(F32) + z_in[0, j, hh].astype(F32)
            vel[j, hh, x, c] = (noisy[j, hh, x, c] + total).astype(BF)
        share_start(0, vel, j)

    for j in range(CH):
        sum_x_start(0, term, j)
    for e in (8, 9, 10, 11):
        w_zstep(1, e)
    for j in range(CH):
        sum_z_start(0, j)
    for e in (12, 13):
        w_zstep(1, e)
    for e in (0, 1, 2, 3, 4, 5, 6, 7):
        w_ystep(1, e)
    own_w[1].wait()
    project(1, 0)
    velocity_rows(0)
    for e in (8, 9, 10, 11):
        w_ystep(1, e)
    velocity_rows(1)
    share_forward(0, vel, 0)
    for e in (12, 13):
        w_ystep(1, e)
    velocity_rows(2)
    share_forward(0, vel, 1)
    velocity_rows(3)
    share_forward(0, vel, 2)
    project_rest(1)

    attend(1)
    share_forward(0, vel, 3)
    for j in range(CH):
        s_term[j] = mm_t(gated[...], out_columns(1, j)).astype(BF).reshape(shape6)

    moved = jnp.zeros((SEQ, 3 * HD), F32)
    inner = jnp.zeros((SEQ, 1), F32)
    for j in range(CH):
        share_wait(0, vel, j)
        arrived = vel[j].reshape(SEQ, CW)
        product = noisy[j].reshape(SEQ, CW) * arrived.astype(F32)
        inner = inner + jnp.sum(product, axis=-1, keepdims=True)
        moved = moved + mm(arrived, w[1, NZ * j : NZ * (j + 1), :, 0 : 3 * HD].reshape(CW, 3 * HD))
    factor = inv[...].reshape(SEQ, HD)[:, :1]
    d_proj = (factor * (moved - factor * inner / D * acc[...])).astype(BF)
    d_queries, d_keys, d_values = (d_proj[:, i * HD : (i + 1) * HD] for i in range(3))
    d_scores = (mm_t(d_queries, proj[:, HD : 2 * HD]) + mm_t(proj[:, :HD], d_keys)) * scale
    probs = att[...]
    d_probs = probs * (d_scores - jnp.sum(probs * d_scores, axis=-1, keepdims=True))
    d_attended = mm(d_probs.astype(BF), proj[:, 2 * HD :]) + mm(att_b[...], d_values)
    d_gated = (d_attended * (1.0 + gates[1:2]) + attended[...] * gates[2:3]).astype(BF)
    for j in range(CH):
        d_term = mm_t(d_gated, out_columns(1, j)).astype(BF).astype(F32)
        cosine, sine = trig[0:1], trig[1:2]
        both = cosine * cosine * s_term[j].reshape(SEQ, CW).astype(F32) + cosine * sine * d_term
        g_term[j] = both.astype(BF).reshape(shape6)
        cs_copy(1, g_term, j).start()

    def gap_rows(j):
        zs_arrival(1, j).wait_recv()
        cosine, sine = trig[0:1], trig[1:2]
        for hh in range(2):
            total = z_sum[1, j, hh].astype(F32) + z_in[1, j, hh].astype(F32)
            clear = -(cosine * cosine + cosine * sine) * noisy[j, hh, x, c]
            moved = (cosine * cosine - cosine * sine) * vel[j, hh, x, c].astype(F32)
            gap[j, hh, x, c] = (clear + moved - total).astype(BF)
        share_start(1, gap, j)

    for j in range(CH):
        sum_x_start(1, g_term, j)
    for j in range(CH):
        cs_copy(2, s_term, j).start()
    for j in range(CH):
        sum_z_start(1, j)
    for j in range(CH):
        sum_x_start(2, s_term, j)
    w_drain(0)
    w_drain(1)
    sum_drain(0, term, vel)
    gap_rows(0)
    gap_rows(1)
    share_forward(1, gap, 0)
    sum_z_start(2, 0)
    sum_z_start(2, 1)
    gap_rows(2)
    share_forward(1, gap, 1)
    sum_z_start(2, 2)
    sum_z_start(2, 3)
    gap_rows(3)
    share_forward(1, gap, 2)
    share_forward(1, gap, 3)

    square = jnp.zeros((1, 1), F32)
    back = jnp.zeros((SEQ, HD), F32)
    for j in range(CH):
        share_wait(1, gap, j)
        whole = gap[j].reshape(SEQ, CW)
        wide = whole.astype(F32)
        rows = jnp.sum(wide * wide, axis=0, keepdims=True)
        square = square + jnp.sum(rows, axis=1, keepdims=True)
        back = back + mm(whole, out_columns(1, j))
    cot = -math.sqrt(D / IMAGES) / (jnp.sqrt(square) + 0.1)
    d_att_b = (back * cot * (1.0 + gates[1:2])).astype(BF)
    queries, keys, values = (proj[:, i * HD : (i + 1) * HD] for i in range(3))
    grad_values = t_mm(att_b[...], d_att_b)
    d_back = mm_t(d_att_b, values)
    probs = att[...]
    d_scores_b = (probs * (d_back - jnp.sum(probs * d_back, axis=-1, keepdims=True)) * scale).astype(BF)
    grad_queries = mm(d_scores_b, keys)
    grad_keys = t_mm(d_scores_b, queries)
    d_proj_b = jnp.concatenate([grad_queries, grad_keys, grad_values], axis=1).astype(BF)

    def gh_copy(d, way):
        part = pl.ds(way * HALF, HALF)
        return rcopy(
            grad.at[(y + 2) % NY, d, part], y_half.at[way, d], gh_s.at[way, d], gh_r.at[way, d], y_to(1 - 2 * way)
        )

    def gf_copy(d, way):
        return rcopy(
            grad.at[(y + 1 - 2 * way + NY) % NY, d],
            y_full.at[way, d],
            gf_s.at[way, d],
            gf_r.at[way, d],
            y_to(1 - 2 * way),
        )

    def gz_copy(d, way):
        dst = z_flow.at[2, 0] if way == 2 else z_flow.at[way, d]
        recv = gz_r.at[2, 0] if way == 2 else gz_r.at[way, d]
        return rcopy(grad.at[y, d], dst, gz_s.at[d], recv, z_to((-1, 1, NG)[way]))

    late_first = (12, 13, 10, 11, 6, 7, 8, 9, 3, 4, 5, 1, 2, 0)

    for k in (2, 1, 3, 0):
        yy = (y + k) % NY
        left = t_mm(normed[yy].reshape(SEQ, CW), d_proj_b)
        grad[yy, :, :, 0 : 3 * HD] = left.astype(BF).reshape(NZ, ROWS, 3 * HD)
        right = t_mm(gap[yy].reshape(SEQ, CW), gated[...]) * cot
        grad[yy, :, :, 3 * HD :] = right.astype(BF).reshape(NZ, ROWS, HD)
        if k == 2:

            for e in late_first:

                @pl.when(events[e][1])
                def _():
                    for way in range(2):
                        gh_copy(events[e][0], way).start()

    def y_second(d):
        for way in range(2):
            gh_copy(d, way).wait_recv()
            yy = (y + 1 - 2 * way + NY) % NY
            part = pl.ds(way * HALF, HALF)
            total = grad[yy, d, part].astype(F32) + y_half[way, d].astype(F32)
            grad[yy, d, part] = total.astype(BF)
            gf_copy(d, way).start()

    for e in late_first:

        @pl.when(events[e][1])
        def _():
            y_second(events[e][0])

    sum_drain(1, g_term, gap)

    for e in late_first:
        d, there, side, right, left = events[e]

        @pl.when(there)
        def _():
            for way in range(2):
                gf_copy(d, way).wait_recv()
            grad[y, d] = (grad[y, d].astype(F32) + y_full[0, d].astype(F32) + y_full[1, d].astype(F32)).astype(BF)
            for way, child in ((0, right), (1, left)):

                @when(child)
                def _():
                    gz_copy(d, way).wait_recv()
                    grad[y, d] = (grad[y, d].astype(F32) + z_flow[way, d].astype(F32)).astype(BF)

            if e:
                gz_copy(d, side).start()
            else:
                gz_copy(d, 2).wait_recv()
                out_g[...] = (grad[y, d].astype(F32) + z_flow[2, 0].astype(F32)).astype(BF)

    sum_drain(2, s_term, None)
    for j in range(CH):
        zs_arrival(2, j).wait_recv()
        total = z_sum[2, j, zh].astype(F32) + z_in[2, j, 1 - zh].astype(F32)
        out_v[:, j * CW : (j + 1) * CW] = (noisy[j, zh, x, c] + total).astype(BF)


    @pl.loop(0, NZ)
    def _(d):
        for way in range(2):
            gh_copy(d, way).wait_send()
            gf_copy(d, way).wait_send()

        @pl.when(d != zl)
        def _():
            gz_copy(d, 0).wait_send()


def on_device(clean, noise, time_index, teacher_w, student_w, teacher_t, student_t):
    blocks = (CH, 2, NX, 2, OWN, CW)
    dma = pltpu.SemaphoreType.DMA
    scratch = [
        pltpu.VMEM((CH, SEQ, CW), BF),
        pltpu.VMEM((CH, SEQ, CW), BF),
        pltpu.VMEM((2,) + teacher_t.shape, BF),
        pltpu.VMEM((2, IMAGES, ROWS, 4 * HD), BF),
        pltpu.VMEM(blocks, F32),
        pltpu.VMEM(blocks, BF),
        pltpu.VMEM((2, NX, 2, OWN, HD), F32),
        pltpu.VMEM((8, CW), F32),
        pltpu.VMEM((8, HD), F32),
        pltpu.VMEM((SEQ, 3 * HD), F32),
        pltpu.VMEM((SEQ, 3 * HD), BF),
        pltpu.VMEM((SEQ, SEQ), F32),
        pltpu.VMEM((SEQ, SEQ), BF),
        pltpu.VMEM((SEQ, HD), F32),
        pltpu.VMEM((SEQ, HD), BF),
        pltpu.VMEM(blocks, BF),
        pltpu.VMEM(blocks, BF),
        pltpu.VMEM(blocks, BF),
        pltpu.VMEM((3, CH, 2, NX, OWN, CW), BF),
        pltpu.VMEM((3, CH, 2, NX, OWN, CW), BF),
        pltpu.VMEM((3, CH, NX - 1, 2, OWN, CW), BF),
        pltpu.VMEM((3, CH, 2, OWN, CW), BF),
        pltpu.VMEM((3, CH, 2, OWN, CW), BF),
        pltpu.VMEM(blocks, BF),
        pltpu.VMEM(blocks, BF),
        pltpu.VMEM((NY, NZ, ROWS, 4 * HD), BF),
        pltpu.VMEM((2, NZ, HALF, 4 * HD), BF),
        pltpu.VMEM((2, NZ, ROWS, 4 * HD), BF),
        pltpu.VMEM((3, NZ, ROWS, 4 * HD), BF),
        dma((2 * CH + 4,)),
        dma((2, NZ, 3)),
        dma((2, NZ)),
        dma((2, NZ, 2, 2)),
        dma((2, NZ, 2, 2)),
        dma((2, NZ, 2)),
        dma((2, NZ, 2)),
        dma((3, CH)),
        dma((3, CH)),
        dma((3, CH, NX - 1)),
        dma((3, CH, NX - 1)),
        dma((3, CH)),
        dma((3, CH)),
        dma((2, CH, NX - 1)),
        dma((2, CH, NX - 1)),
        dma((2, CH, NX)),
        dma((2, CH, NX)),
        dma((2, NZ)),
        dma((2, NZ)),
        dma((2, NZ)),
        dma((2, NZ)),
        dma((NZ,)),
        dma((3, NZ)),
    ]
    out_v, out_g = pl.pallas_call(
        kernel,
        name="distill_step",
        out_shape=(jax.ShapeDtypeStruct((OWN, D), BF), jax.ShapeDtypeStruct((ROWS, 4 * HD), BF)),
        in_specs=[pl.BlockSpec(memory_space=pltpu.SMEM)] + [pl.BlockSpec(memory_space=pl.ANY)] * 6,
        out_specs=(pl.BlockSpec(memory_space=pltpu.VMEM), pl.BlockSpec(memory_space=pltpu.VMEM)),
        scratch_shapes=scratch,
        compiler_params=pltpu.CompilerParams(
            collective_id=0, has_side_effects=True, vmem_limit_bytes=60 * 1024 * 1024
        ),
        cost_estimate=pl.CostEstimate(flops=4_000_000_000, bytes_accessed=4_000_000, transcendentals=200_000),
    )(time_index, clean[0], noise[0], teacher_w, student_w, teacher_t, student_t)
    return (out_v[None], out_g)


def solution(mesh):
    placed = (
        P("dp", None, None),
        P("dp", None, None),
        P("dp"),
        P("dp", "tp"),
        P("dp", "tp"),
        P(None, "tp"),
        P(None, "tp"),
    )
    return jax.shard_map(
        on_device,
        mesh=mesh,
        in_specs=placed,
        out_specs=(P("dp", "tp", None), P("dp", "tp")),
        check_vma=False,
    )
```
